128 devices in a mesh: worker: 8 (over y, z_hi), fsdp: 16 (over z_lo, x, core).
Axes of the slice: x: 4, y: 4, z: 4 (z_hi: 2, z_lo: 2; z = z_hi * 2 + z_lo), core: 2. Of those that a mesh axis runs over, the one named last changes fastest.
Arguments:
- local_params: float32 [8, 4096, 8192], P('worker', None, 'fsdp'), may hold values from -6 to 6
- global_params: float32 [4096, 8192], P(('worker', 'fsdp')), may hold values from -6 to 6
- momentum: float32 [4096, 8192], P(('worker', 'fsdp')), may hold values from -3 to 3
- step_counts: int32 [8], P('worker'), may hold values from 64 to 256
- alive: int32 [8], P('worker'), may hold values from 0 to 1, as said below
Outputs:
- new_params: float32 [4096, 8192], P(None, 'fsdp')
- new_momentum: float32 [4096, 8192], P(('worker', 'fsdp'))
The draws below stay inside these ranges and needn't reach their ends.
Inputs may be any that keep to these rules, and one draw needn't show every extreme that they name: Exactly one worker has alive 0.
All inputs are finite; a program needn't handle non-finite values.
Results may differ from the reference program's by a relative error of at most 0.00007.
Values sent between devices are 32-bit elements; how exact they have to be, the bound alone decides.
A program may use at most 128 MiB of HBM per device.

```python
import jax
import jax.numpy as jnp

D = 8192
WORKERS = 8
ROWS = 4096


def draw_alive(key, part):
    key = jax.random.fold_in(key, 5)
    failed = jax.random.randint(key, (), 0, WORKERS)
    return (jnp.arange(WORKERS, dtype=jnp.int32) != failed).astype(jnp.int32)


def touch_ends(drawn, own_key, low, high):
    dims = drawn.shape
    place = [jax.random.randint(jax.random.fold_in(own_key, axis), (), 0, dims[axis]) for axis in range(len(dims))]
    drawn = drawn.at[tuple(place)].set(low)
    longest = dims.index(max(dims))
    place[longest] = (place[longest] + 1) % dims[longest]
    return drawn.at[tuple(place)].set(high)


def level_of(stream_key, dims, split, least, largest):
    loudness, own = 1.0, jax.random.fold_in(stream_key, 6)
    for dim, parts in split:
        draws = jnp.exp(jax.random.uniform(jax.random.fold_in(own, dim), (parts,), jnp.float32, least / len(split), largest / len(split)))
        loudness = loudness * jnp.repeat(draws, dims[dim] // parts).reshape([-1 if axis == dim else 1 for axis in range(len(dims))])
    return loudness


def noise(key, dims, width, limit, cuts=(), kind=jnp.bfloat16):
    array = width * jax.random.normal(key, dims, jnp.float32)
    if cuts:
        array = array * level_of(key, dims, cuts, -0.22, 0.18)
    return jnp.clip(array, -limit, limit).astype(kind)


def setup_inputs(seed: int = 0) -> dict:
    seeds = jax.random.split(jax.random.key(seed), 6)
    local_params = noise(seeds[0], (WORKERS, ROWS, D), 1.0, 6.0, ((0, 8), (2, 16)), jnp.float32)
    global_params = noise(seeds[1], (ROWS, D), 1.0, 6.0, ((0, 128),), jnp.float32)
    momentum = noise(seeds[2], (ROWS, D), 0.5, 3.0, ((0, 128),), jnp.float32)
    step_counts = touch_ends(jax.random.randint(seeds[3], (WORKERS,), 64, 257), jax.random.fold_in(seeds[3], 1), 64, 256).astype(jnp.int32)
    alive = draw_alive(jax.random.fold_in(seeds[5], 71), 0)
    return {"local_params": local_params, "global_params": global_params, "momentum": momentum, "step_counts": step_counts, "alive": alive}


def reference(local_params, global_params, momentum, step_counts, alive):
    weight = (step_counts * alive).astype(jnp.float32)
    total = jnp.sum(weight)
    summed = jnp.tensordot(weight, local_params, axes=1)
    average = summed / total
    outer_grad = global_params - average
    new_momentum = 0.9 * momentum + outer_grad
    new_params = global_params - 0.7 * (outer_grad + 0.9 * new_momentum)
    return new_params, new_momentum
```

```python
import functools

import jax
import jax.numpy as jnp
from jax import lax
from jax.experimental import pallas as pl
from jax.experimental.pallas import tpu as pltpu
from jax.sharding import PartitionSpec as P

MESH = pl.DeviceIdType.MESH
F32 = jnp.float32

A = (64, 64, 64, 64, 64, 32,)
B = (64, 64, 32,)
ORDER = [(c[0], c[1], int(c[2])) for c in (
    "LA0", "LB0", "LA1", "CA0", "FB0", "LB1", "LA2", "CA1", "ZA0", "CB0", "CA2", "LB2",
    "ZA1", "LA3", "FB1", "H00", "LA4", "LA5", "ZA2", "FB2", "CA3", "CA4", "CA5", "ZA3",
    "CB1", "NB0", "ZA4", "NA0", "ZA5", "NA1", "NB1", "XB0", "PA0", "CB2", "PA1", "XB1",
    "XA0", "YB0", "XA1", "YA0", "NB2", "NA2", "YB1", "YA1", "NA3", "EB0", "EA0", "XB2",
    "PA2", "XA2", "EA1", "NA4", "EB1", "NA5", "YB2", "PA3", "V00", "YA2", "XA3", "PA4",
    "EB2", "PA5", "XA4", "YA3", "EA2", "XA5", "YA4", "YA5", "M00", "EA3", "EA4", "EA5",
)]


def pieces():
    at, out = 0, {}
    for kind, sizes in (("A", A), ("B", B)):
        for p, n in enumerate(sizes):
            out[kind, p] = (at, n)
            at += n
    return out


PIECES = pieces()
TAGS = {
    "A": ("fr", "fl", "cr", "cl", "z", "gz", "gr", "gl", "pr", "pl", "xr", "xl", "yr", "yl"),
    "B": ("zb0", "zb1", "zb2", "zb3", "fr", "fl", "cr", "cl", "gr", "gl", "xr", "xl", "gz0", "gz1", "gz2", "gz3"),
}
INDEX = {key: i for i, key in enumerate((t, k, p) for (k, p) in PIECES for t in TAGS[k])}


def kernel(
    local_ref, g_hbm, m_hbm, steps_ref, alive_ref, out, nm_out,
    work, rf, rcl, rcr, rz, g, m, hs, hr, av, avr, wt, inv,
    load_sem, gm_sem, send_sem, recv_sem, wt_send, wt_recv, h_send, h_recv, v_send, v_recv,
):
    w, f = lax.axis_index("worker"), lax.axis_index("fsdp")
    y, zh = w // 2, w % 2
    zo = 1 - zh
    yr, yl, y2 = (y + 1) % 4, (y + 3) % 4, (y + 2) % 4
    right, left, over = (yr * 2 + zh, f), (yl * 2 + zh, f), (y * 2 + zo, f)

    def load(key):
        at, n = PIECES[key]
        rows = pl.ds(at, n)
        i = list(PIECES).index(key)
        return pltpu.make_async_copy(local_ref.at[:, :, rows], work.at[:, :, rows], load_sem.at[i])

    lorder = [(k, p) for s, k, p in ORDER if s == "L"]
    for key in lorder[:2]:
        load(key).start()
    g_copy = pltpu.make_async_copy(g_hbm, g, gm_sem.at[0])
    m_copy = pltpu.make_async_copy(m_hbm, m, gm_sem.at[1])
    g_copy.start()
    m_copy.start()
    for key in lorder[2:]:
        load(key).start()

    barrier = pltpu.get_barrier_semaphore()

    def greet_worker(d, c):
        pl.semaphore_signal(barrier, inc=1, device_id=((w + d) % 8, f), device_id_type=MESH)
        return c

    def greet_fsdp(d, c):
        pl.semaphore_signal(barrier, inc=1, device_id=(w, (f + d) % 16), device_id_type=MESH)
        return c

    lax.fori_loop(1, 8, greet_worker, 0)
    lax.fori_loop(1, 16, greet_fsdp, 0)

    weight = (steps_ref[0] * alive_ref[0]).astype(F32)

    def channel(tag, kind, p):
        at, n = PIECES[kind, p]
        half = n // 2
        rows, lo, hi = pl.ds(at, n), pl.ds(at, half), pl.ds(at + half, half)
        if tag[:2] == "zb":
            t = {"0": y, "1": yr, "2": y2, "3": yl}[tag[2]]
            return work.at[t, zo, rows], rz.at[t, rows], over, rz.at[t, rows]
        if tag == "z":
            return work.at[y, zo, rows], rz.at[0, rows], over, rz.at[0, rows]
        if tag in ("fr", "fl", "cr", "cl"):
            z, q = (slice(None), slice(None)) if kind == "A" else (zh, 0)
            if tag == "fr":
                return work.at[y2, z, lo], rf.at[q, lo], right, rf.at[q, lo]
            if tag == "fl":
                return work.at[y2, z, hi], rf.at[q, hi], left, rf.at[q, hi]
            if tag == "cr":
                return work.at[yr, z, rows], rcl.at[q, rows], right, rcl.at[q, rows]
            return work.at[yl, z, rows], rcr.at[q, rows], left, rcr.at[q, rows]
        if tag[:2] == "gz":
            t = {"": y, "0": y, "1": yl, "2": y2, "3": yr}[tag[2:]]
            return out.at[t, zh, rows], out.at[t, zh, rows], over, out.at[t, zo, rows]
        z = zo if tag[0] in "py" else zh
        if tag in ("gr", "pr"):
            return out.at[y, z, rows], out.at[y, z, rows], right, out.at[yl, z, rows]
        if tag in ("gl", "pl"):
            return out.at[y, z, rows], out.at[y, z, rows], left, out.at[yr, z, rows]
        if tag in ("xr", "yr"):
            return out.at[yl, z, lo], out.at[yl, z, lo], right, out.at[y2, z, lo]
        return out.at[yr, z, hi], out.at[yr, z, hi], left, out.at[y2, z, hi]

    sent = []

    def send(tag, kind, p):
        src, dst, device, _ = channel(tag, kind, p)
        i = INDEX[tag, kind, p]
        copy = pltpu.make_async_remote_copy(
            src, dst, send_sem.at[i], recv_sem.at[i], device_id=device, device_id_type=MESH
        )
        copy.start()
        sent.append(copy)

    def wait(tag, kind, p):
        src, _, device, land = channel(tag, kind, p)
        i = INDEX[tag, kind, p]
        pltpu.make_async_remote_copy(
            src, land, send_sem.at[i], recv_sem.at[i], device_id=device, device_id_type=MESH
        ).wait_recv()

    def weigh(key):
        at, n = PIECES[key]
        load(key).wait()

        def body(i, c):
            ref = work.at[i // 2, i % 2, pl.ds(at, n)]
            ref[...] = ref[...] * weight
            return c

        lax.fori_loop(0, 8, body, 0)

    def wt_copy(d):
        to, source = (w + d) % 8, (w + 8 - d) % 8
        return pltpu.make_async_remote_copy(
            wt.at[w], wt.at[w], wt_send.at[d], wt_recv.at[d], device_id=(to, f), device_id_type=MESH
        ), pltpu.make_async_remote_copy(
            wt.at[w], wt.at[source], wt_send.at[d], wt_recv.at[d], device_id=(to, f), device_id_type=MESH
        )

    def h_copy(d):
        to, source = (f + d) % 16, (f + 16 - d) % 16
        dst = hr.at[pl.ds(pl.multiple_of(32 * f, 32), 32)]
        land = hr.at[pl.ds(pl.multiple_of(32 * source, 32), 32)]
        return tuple(
            pltpu.make_async_remote_copy(
                hs.at[to], t, h_send.at[d], h_recv.at[d], device_id=(w, to), device_id_type=MESH
            )
            for t in (dst, land)
        )

    def v_copy(d):
        to, source = (f + d) % 16, (f + 16 - d) % 16
        src = av.at[pl.ds(pl.multiple_of(32 * to, 32), 32)]
        return tuple(
            pltpu.make_async_remote_copy(
                src, t, v_send.at[d], v_recv.at[d], device_id=(w, to), device_id_type=MESH
            )
            for t in (avr.at[f], avr.at[source])
        )

    def each(copies, n, what):
        def body(d, c):
            out_copy, in_copy = copies(d)
            if what == "start":
                out_copy.start()
            elif what == "recv":
                in_copy.wait_recv()
            else:
                out_copy.wait_send()
            return c

        lax.fori_loop(1, n, body, 0)

    ready = []

    def need_h():
        if ready:
            return
        ready.append(True)
        each(wt_copy, 8, "recv")
        total = wt[0]
        for i in range(1, 8):
            total = total + wt[i]
        inv[...] = 1.0 / total
        each(h_copy, 16, "recv")

    def finish(at, n, s):
        rows = pl.ds(at, n)
        average = s * inv[0:1, :]
        av[rows] = average
        out[y, zh, rows] = 1.33 * average + hr[rows]

    entered = []
    for step, kind, p in ORDER:
        if step == "H":
            g_copy.wait()
            m_copy.wait()
            for i in range(16):
                cols = pl.ds(512 * i, 512)
                hs[i] = -0.33 * g[:, cols] - 0.567 * m[:, cols]
            hr[pl.ds(pl.multiple_of(32 * f, 32), 32)] = hs[f]
            each(h_copy, 16, "start")
            continue
        if step == "V":
            avr[f] = av[pl.ds(pl.multiple_of(32 * f, 32), 32)]
            each(v_copy, 16, "start")
            continue
        if step == "M":
            each(v_copy, 16, "recv")
            for i in range(16):
                cols = pl.ds(512 * i, 512)
                nm_out[:, cols] = 0.9 * m[:, cols] + (g[:, cols] - avr[i])
            continue
        at, n = PIECES[kind, p]
        half = n // 2
        rows, lo, hi = pl.ds(at, n), pl.ds(at, half), pl.ds(at + half, half)
        if step == "L":
            weigh((kind, p))
            if not entered:
                entered.append(True)
                wt[w] = jnp.full((8, 512), weight, F32)
                pl.semaphore_wait(barrier, 22)
                each(wt_copy, 8, "start")
            for tag in ("fr", "fl") if kind == "A" else ("zb2", "zb1", "zb3", "zb0"):
                send(tag, kind, p)
        elif step == "F":
            wait("zb2", kind, p)
            work[y2, zh, rows] += rz[y2, rows]
            send("fr", kind, p)
            send("fl", kind, p)
        elif step == "C":
            wait("fr", kind, p)
            wait("fl", kind, p)
            if kind == "A":
                for z in range(2):
                    work[yr, z, lo] += rf[z, lo]
                    work[yl, z, hi] += rf[z, hi]
            else:
                wait("zb1", kind, p)
                wait("zb3", kind, p)
                work[yr, zh, lo] += rz[yr, lo] + rf[0, lo]
                work[yr, zh, hi] += rz[yr, hi]
                work[yl, zh, lo] += rz[yl, lo]
                work[yl, zh, hi] += rz[yl, hi] + rf[0, hi]
            send("cr", kind, p)
            send("cl", kind, p)
        elif step == "Z":
            wait("cr", kind, p)
            wait("cl", kind, p)
            for z in range(2):
                work[y, z, rows] += rcl[z, rows] + rcr[z, rows]
            send("z", kind, p)
        elif step == "N":
            if kind == "A":
                wait("z", kind, p)
                need_h()
                finish(at, n, work[y, zh, rows] + rz[0, rows])
                for tag in ("gz", "gr", "gl"):
                    send(tag, kind, p)
            else:
                wait("cr", kind, p)
                wait("cl", kind, p)
                wait("zb0", kind, p)
                need_h()
                finish(at, n, work[y, zh, rows] + rz[y, rows] + rcl[0, rows] + rcr[0, rows])
                for tag in ("gr", "gl", "gz0"):
                    send(tag, kind, p)
        elif step == "P":
            wait("gz", kind, p)
            send("pr", kind, p)
            send("pl", kind, p)
        elif step == "X":
            wait("gr", kind, p)
            wait("gl", kind, p)
            send("xr", kind, p)
            send("xl", kind, p)
            if kind == "B":
                send("gz1", kind, p)
                send("gz3", kind, p)
        elif step == "Y":
            if kind == "A":
                wait("pr", kind, p)
                wait("pl", kind, p)
                send("yr", kind, p)
                send("yl", kind, p)
            else:
                wait("xr", kind, p)
                wait("xl", kind, p)
                send("gz2", kind, p)
        elif step == "E":
            for tag in ("xr", "xl", "yr", "yl") if kind == "A" else ("gz0", "gz1", "gz3", "gz2"):
                wait(tag, kind, p)

    for copy in sent:
        copy.wait_send()
    each(wt_copy, 8, "sent")
    each(h_copy, 16, "sent")
    each(v_copy, 16, "sent")


def local(local_params, global_params, momentum, step_counts, alive):
    hbm = pl.BlockSpec(memory_space=pltpu.HBM)
    smem = pl.BlockSpec(memory_space=pltpu.SMEM)
    n = len(INDEX)
    dma = pltpu.SemaphoreType.DMA
    out, nm = pl.pallas_call(
        kernel,
        out_shape=(pltpu.VMEM((4, 2, 512, 512), F32), pltpu.VMEM((32, 8192), F32)),
        in_specs=[hbm, hbm, hbm, smem, smem],
        out_specs=(pl.BlockSpec(memory_space=pltpu.VMEM), pl.BlockSpec(memory_space=pltpu.VMEM)),
        scratch_shapes=[
            pltpu.VMEM((4, 2, 512, 512), F32),
            pltpu.VMEM((2, 512, 512), F32),
            pltpu.VMEM((2, 512, 512), F32),
            pltpu.VMEM((2, 512, 512), F32),
            pltpu.VMEM((4, 512, 512), F32),
            pltpu.VMEM((32, 8192), F32),
            pltpu.VMEM((32, 8192), F32),
            pltpu.VMEM((16, 32, 512), F32),
            pltpu.VMEM((512, 512), F32),
            pltpu.VMEM((512, 512), F32),
            pltpu.VMEM((16, 32, 512), F32),
            pltpu.VMEM((8, 8, 512), F32),
            pltpu.VMEM((8, 512), F32),
            dma((len(PIECES),)),
            dma((2,)),
            dma((n,)),
            dma((n,)),
            dma((8,)),
            dma((8,)),
            dma((16,)),
            dma((16,)),
            dma((16,)),
            dma((16,)),
        ],
        compiler_params=pltpu.CompilerParams(
            collective_id=0, has_side_effects=True, vmem_limit_bytes=48 << 20
        ),
        name="outer_step",
    )(local_params.reshape(4, 2, 512, 512), global_params, momentum, step_counts, alive)
    return out.reshape(4096, 512), nm


def solution(mesh):
    in_specs = (
        P("worker", None, "fsdp"),
        P(("worker", "fsdp"), None),
        P(("worker", "fsdp"), None),
        P("worker"),
        P("worker"),
    )
    out_specs = (P(None, "fsdp"), P(("worker", "fsdp"), None))
    return jax.shard_map(local, mesh=mesh, in_specs=in_specs, out_specs=out_specs, check_vma=False)
```

```python
import functools

import jax
import jax.numpy as jnp
from jax import lax
from jax.experimental import pallas as pl
from jax.experimental.pallas import tpu as pltpu
from jax.sharding import PartitionSpec as P

MESH = pl.DeviceIdType.MESH
F32 = jnp.float32

A = ((0, 4, 0, 16), (4, 4, 0, 16), (8, 4, 0, 16), (12, 4, 0, 16), (0, 8, 16, 8),)
B = ((8, 4, 16, 16), (12, 4, 16, 16), (0, 8, 24, 8),)
ORDER = [(c[0], c[1], int(c[2])) for c in (
    "LA0", "LB0", "LA1", "CA0", "FB0", "H00", "CA1", "LB1", "LA2", "CB0", "FB1", "CA2",
    "LB2", "LA3", "ZA0", "ZA1", "LA4", "CB1", "ZA2", "FB2", "CA3", "CA4", "NA0", "ZA3",
    "NA1", "NA2", "GA0", "ZA4", "CB2", "NA3", "GA1", "NB0", "GA2", "NB1", "NA4", "GA3",
    "U00", "XA0", "GB0", "XA1", "NB2", "GB1", "V00", "XA2", "GA4", "XA3", "XA4", "XB0",
    "PA0", "GB2", "XB1", "PA1", "PA2", "YB0", "PA3", "M00", "YB1", "YA0", "XB2", "YA1",
    "PA4", "EB0", "YA2", "EB1", "YA3", "EA0", "YB2", "EA1", "YA4", "EA2", "EB2", "EA3",
    "EA4",
)]


PIECES = {(kind, p): piece for kind, sizes in (("A", A), ("B", B)) for p, piece in enumerate(sizes)}


def part(key):
    f, nf, r, nr = PIECES[key]
    rows = pl.ds(r, nr)
    return (pl.ds(f, nf), rows), (pl.ds(f, nf // 2), rows), (pl.ds(f + nf // 2, nf // 2), rows)


LAG = 24
TAGS = {
    "A": ("fr", "fl", "cr", "cl", "z", "gz", "gr", "gl", "pr", "pl", "xr", "xl", "yr", "yl"),
    "B": ("zb0", "zb1", "zb2", "zb3", "fr", "fl", "cr", "cl", "gr", "gl", "xr", "xl", "gz0", "gz1", "gz2", "gz3"),
}
INDEX = {key: i for i, key in enumerate((t, k, p) for (k, p) in PIECES for t in TAGS[k])}


def kernel(
    local_ref, g_hbm, m_hbm, steps_hbm, alive_hbm, out, nm_out,
    work, rf, rcl, rcr, rz, g, m, hs, hr, hp, avr, wt, inv, scale, steps_ref, alive_ref,
    load_sem, gm_sem, send_sem, recv_sem, wt_send, wt_recv, h_send, h_recv, v_send, v_recv,
):
    w, f = lax.axis_index("worker"), lax.axis_index("fsdp")
    y, zh = w // 2, w % 2
    zo = 1 - zh
    yr, yl, y2 = (y + 1) % 4, (y + 3) % 4, (y + 2) % 4
    zl, fl = f // 8, f % 8

    def across(d):
        return y * 2 + zo, (1 - zl) * 8 + (fl + d) % 8

    right, left, over = (yr * 2 + zh, f), (yl * 2 + zh, f), (y * 2 + zo, f)

    def load(key):
        rows = part(key)[0]
        i = list(PIECES).index(key)
        return pltpu.make_async_copy(local_ref.at[:, :, *rows], work.at[:, :, *rows], load_sem.at[i])

    lorder = [(k, p) for s, k, p in ORDER if s == "L"]
    for key in lorder[:2]:
        load(key).start()
    steps_copy = pltpu.make_async_copy(steps_hbm, steps_ref, gm_sem.at[2])
    alive_copy = pltpu.make_async_copy(alive_hbm, alive_ref, gm_sem.at[3])
    steps_copy.start()
    alive_copy.start()
    g_copy = pltpu.make_async_copy(g_hbm, g, gm_sem.at[0])
    m_copy = pltpu.make_async_copy(m_hbm, m, gm_sem.at[1])

    barrier = pltpu.get_barrier_semaphore()

    def greet_worker(d, c):
        pl.semaphore_signal(barrier, inc=1, device_id=((w + d) % 8, f), device_id_type=MESH)
        return c

    def greet_fsdp(d, c):
        pl.semaphore_signal(barrier, inc=1, device_id=(w, (f + d) % 16), device_id_type=MESH)
        return c

    def greet_across(d, c):
        pl.semaphore_signal(barrier, inc=1, device_id=across(d), device_id_type=MESH)
        return c

    lax.fori_loop(1, 8, greet_worker, 0)
    lax.fori_loop(1, 16, greet_fsdp, 0)
    lax.fori_loop(0, 8, greet_across, 0)
    g_copy.start()
    m_copy.start()
    for key in lorder[2:]:
        load(key).start()
    steps_copy.wait()
    alive_copy.wait()

    weight = (steps_ref[0] * alive_ref[0]).astype(F32)

    def channel(tag, kind, p):
        rows, lo, hi = part((kind, p))
        if tag[:2] == "zb":
            t = {"0": y, "1": yr, "2": y2, "3": yl}[tag[2]]
            return work.at[t, zo, *rows], rz.at[t, *rows], over, rz.at[t, *rows]
        if tag == "z":
            return work.at[y, zo, *rows], rz.at[0, *rows], over, rz.at[0, *rows]
        if tag in ("fr", "fl", "cr", "cl"):
            z, q = (slice(None), slice(None)) if kind == "A" else (zh, 0)
            if tag == "fr":
                return work.at[y2, z, *lo], rf.at[q, *lo], right, rf.at[q, *lo]
            if tag == "fl":
                return work.at[y2, z, *hi], rf.at[q, *hi], left, rf.at[q, *hi]
            if tag == "cr":
                return work.at[yr, z, *rows], rcl.at[q, *rows], right, rcl.at[q, *rows]
            return work.at[yl, z, *rows], rcr.at[q, *rows], left, rcr.at[q, *rows]
        if tag[:2] == "gz":
            t = {"": y, "0": y, "1": yl, "2": y2, "3": yr}[tag[2:]]
            return out.at[t, zh, *rows], out.at[t, zh, *rows], over, out.at[t, zo, *rows]
        z = zo if tag[0] in "py" else zh
        if tag in ("gr", "pr"):
            return out.at[y, z, *rows], out.at[y, z, *rows], right, out.at[yl, z, *rows]
        if tag in ("gl", "pl"):
            return out.at[y, z, *rows], out.at[y, z, *rows], left, out.at[yr, z, *rows]
        if tag in ("xr", "yr"):
            return out.at[yl, z, *lo], out.at[yl, z, *lo], right, out.at[y2, z, *lo]
        return out.at[yr, z, *hi], out.at[yr, z, *hi], left, out.at[y2, z, *hi]

    sent = []

    def send(tag, kind, p):
        src, dst, device, _ = channel(tag, kind, p)
        i = INDEX[tag, kind, p]
        copy = pltpu.make_async_remote_copy(
            src, dst, send_sem.at[i], recv_sem.at[i], device_id=device, device_id_type=MESH
        )
        copy.start()
        sent.append((now, copy))

    def wait(tag, kind, p):
        src, _, device, land = channel(tag, kind, p)
        i = INDEX[tag, kind, p]
        pltpu.make_async_remote_copy(
            src, land, send_sem.at[i], recv_sem.at[i], device_id=device, device_id_type=MESH
        ).wait_recv()

    def weigh(key):
        rows = part(key)[0]
        load(key).wait()

        def body(i, c):
            ref = work.at[i // 2, i % 2, *rows]
            ref[...] = ref[...] * weight
            return c

        lax.fori_loop(0, 8, body, 0)

    def wt_copy(d):
        to, source = (w + d) % 8, (w + 8 - d) % 8
        return pltpu.make_async_remote_copy(
            wt.at[w], wt.at[w], wt_send.at[d], wt_recv.at[d], device_id=(to, f), device_id_type=MESH
        ), pltpu.make_async_remote_copy(
            wt.at[w], wt.at[source], wt_send.at[d], wt_recv.at[d], device_id=(to, f), device_id_type=MESH
        )

    def near(d):
        return zl * 8 + (fl + d) % 8, zl * 8 + (fl + 8 - d) % 8

    def cross(d):
        return (1 - zl) * 8 + (fl + d) % 8, (1 - zl) * 8 + (fl + 8 - d) % 8

    def both(src, dst, land, send, recv, i, device):
        return tuple(
            pltpu.make_async_remote_copy(
                src, t, send.at[i], recv.at[i], device_id=device, device_id_type=MESH
            )
            for t in (dst, land)
        )

    first, last = pl.ds(0, 16), pl.ds(16, 16)

    def h_near(d):
        to, source = near(d)
        return both(hs.at[to], hr.at[f], hr.at[source], h_send, h_recv, d, (w, to))

    def h_cross(d):
        to, source = cross(d)
        return both(
            hs.at[to, last], hr.at[f, last], hr.at[source, last], h_send, h_recv, 8 + d, (w, to)
        )

    def h_over(d):
        to, source = cross(d)
        return both(hs.at[to, first], hp.at[f], hp.at[source], h_send, h_recv, 16 + d, across(d))

    def v_near(d):
        to, source = near(d)
        return both(out.at[y, zh, to], avr.at[f], avr.at[source], v_send, v_recv, d, (w, to))

    def v_cross(d):
        to, source = cross(d)
        return both(
            out.at[y, zh, to, last], avr.at[f, last], avr.at[source, last],
            v_send, v_recv, 8 + d, (w, to),
        )

    def v_over(d):
        to, source = cross(d)
        return both(
            out.at[y, zo, to, first], avr.at[f, first], avr.at[source, first],
            v_send, v_recv, 16 + d, across(d),
        )

    def each(copies, n, what, first=1):
        def body(d, c):
            out_copy, in_copy = copies(d)
            if what == "start":
                out_copy.start()
            elif what == "recv":
                in_copy.wait_recv()
            else:
                out_copy.wait_send()
            return c

        lax.fori_loop(first, n, body, 0)

    ready = []

    def need_h():
        if ready:
            return
        ready.append(True)
        each(wt_copy, 8, "recv")
        total = wt[0]
        for i in range(1, 8):
            total = total + wt[i]
        inv[...] = 1.33 / total
        scale[...] = total / 1.33
        each(h_near, 8, "recv")
        each(h_cross, 8, "recv", 0)
        each(h_over, 8, "recv", 0)

    def finish(rows, s):
        out[y, zh, *rows] = s * inv[0:1, :] + hr[*rows]

    entered = []
    for now, (step, kind, p) in enumerate(ORDER):
        while sent and sent[0][0] < now - LAG:
            sent.pop(0)[1].wait_send()
        if step == "H":
            g_copy.wait()
            m_copy.wait()
            for i in range(16):
                cols = pl.ds(512 * i, 512)
                hs[i] = -0.33 * g[:, cols] - 0.567 * m[:, cols]
            hr[f] = hs[f]
            hr[pl.ds((1 - zl) * 8, 8), first] = jnp.zeros((8, 16, 512), F32)
            hp[pl.ds(zl * 8, 8)] = jnp.zeros((8, 16, 512), F32)
            each(h_cross, 8, "start", 0)
            each(h_over, 8, "start", 0)
            each(h_near, 8, "start")
            continue
        if step == "V":
            avr[f] = out[y, zh, f]
            each(v_cross, 8, "start", 0)
            each(v_near, 8, "start")
            continue
        if step == "U":
            each(v_over, 8, "start", 0)
            continue
        if step == "M":
            each(v_near, 8, "recv")
            each(v_cross, 8, "recv", 0)
            each(v_over, 8, "recv", 0)
            each(wt_copy, 8, "sent")
            for copies in (h_near, v_near):
                each(copies, 8, "sent")
            for copies in (h_cross, h_over, v_cross, v_over):
                each(copies, 8, "sent", 0)
            for i in range(16):
                cols = pl.ds(512 * i, 512)
                average = (avr[i] + 0.33 * g[:, cols] + 0.567 * m[:, cols]) * (1 / 1.33)
                nm_out[:, cols] = 0.9 * m[:, cols] + (g[:, cols] - average)
            continue
        rows, lo, hi = part((kind, p))
        if step == "L":
            weigh((kind, p))
            if not entered:
                entered.append(True)
                wt[w] = jnp.full((8, 512), weight, F32)
                pl.semaphore_wait(barrier, 30)
                each(wt_copy, 8, "start")
            for tag in ("fr", "fl") if kind == "A" else ("zb2", "zb1", "zb3", "zb0"):
                send(tag, kind, p)
        elif step == "F":
            wait("zb2", kind, p)
            work[y2, zh, *rows] += rz[y2, *rows]
            send("fr", kind, p)
            send("fl", kind, p)
        elif step == "C":
            wait("fr", kind, p)
            wait("fl", kind, p)
            if kind == "A":
                for z in range(2):
                    work[yr, z, *lo] += rf[z, *lo]
                    work[yl, z, *hi] += rf[z, *hi]
            else:
                wait("zb1", kind, p)
                wait("zb3", kind, p)
                work[yr, zh, *lo] += rz[yr, *lo] + rf[0, *lo]
                work[yr, zh, *hi] += rz[yr, *hi]
                work[yl, zh, *lo] += rz[yl, *lo]
                work[yl, zh, *hi] += rz[yl, *hi] + rf[0, *hi]
            send("cr", kind, p)
            send("cl", kind, p)
        elif step == "Z":
            wait("cr", kind, p)
            wait("cl", kind, p)
            for z in range(2):
                work[y, z, *rows] += rcl[z, *rows] + rcr[z, *rows]
            fs, fn, r, _ = PIECES[kind, p]
            if r < 16:
                need_h()
                work[y, zo, *rows] += hp[fs : fs + fn] * scale[0:1, :]
            send("z", kind, p)
        elif step == "N":
            if kind == "A":
                wait("z", kind, p)
                need_h()
                finish(rows, work[y, zh, *rows] + rz[0, *rows])
                for tag in ("gz", "gr", "gl"):
                    send(tag, kind, p)
            else:
                wait("cr", kind, p)
                wait("cl", kind, p)
                wait("zb0", kind, p)
                need_h()
                finish(rows, work[y, zh, *rows] + rz[y, *rows] + rcl[0, *rows] + rcr[0, *rows])
                for tag in ("gr", "gl", "gz0"):
                    send(tag, kind, p)
        elif step == "P":
            send("pr", kind, p)
            send("pl", kind, p)
        elif step == "X":
            wait("gr", kind, p)
            wait("gl", kind, p)
            send("xr", kind, p)
            send("xl", kind, p)
            if kind == "B":
                send("gz1", kind, p)
                send("gz3", kind, p)
        elif step == "Y":
            if kind == "A":
                wait("pr", kind, p)
                wait("pl", kind, p)
                send("yr", kind, p)
                send("yl", kind, p)
            else:
                wait("xr", kind, p)
                wait("xl", kind, p)
                send("gz2", kind, p)
        elif step == "G":
            wait("gz0" if kind == "B" else "gz", kind, p)
        elif step == "E":
            for tag in ("xr", "xl", "yr", "yl") if kind == "A" else ("gz1", "gz3", "gz2"):
                wait(tag, kind, p)

    for _, copy in sent:
        copy.wait_send()


def store(a_ref, b_ref, a_out, b_out, sem):
    copies = [pltpu.make_async_copy(a_ref.at[i // 2, i % 2], a_out.at[i // 2, i % 2], sem.at[i]) for i in range(8)]
    copies.append(pltpu.make_async_copy(b_ref, b_out, sem.at[8]))
    for copy in copies:
        copy.start()
    for copy in copies:
        copy.wait()


def local(local_params, global_params, momentum, step_counts, alive):
    hbm = pl.BlockSpec(memory_space=pltpu.HBM)
    n = len(INDEX)
    dma = pltpu.SemaphoreType.DMA
    out, nm = pl.pallas_call(
        kernel,
        out_shape=(pltpu.VMEM((4, 2, 16, 32, 512), F32), pltpu.VMEM((32, 8192), F32)),
        in_specs=[hbm] * 5,
        out_specs=(pl.BlockSpec(memory_space=pltpu.VMEM), pl.BlockSpec(memory_space=pltpu.VMEM)),
        scratch_shapes=[
            pltpu.VMEM((4, 2, 16, 32, 512), F32),
            pltpu.VMEM((2, 16, 32, 512), F32),
            pltpu.VMEM((2, 16, 32, 512), F32),
            pltpu.VMEM((2, 16, 32, 512), F32),
            pltpu.VMEM((4, 16, 32, 512), F32),
            pltpu.VMEM((32, 8192), F32),
            pltpu.VMEM((32, 8192), F32),
            pltpu.VMEM((16, 32, 512), F32),
            pltpu.VMEM((16, 32, 512), F32),
            pltpu.VMEM((16, 16, 512), F32),
            pltpu.VMEM((16, 32, 512), F32),
            pltpu.VMEM((8, 8, 512), F32),
            pltpu.VMEM((8, 512), F32),
            pltpu.VMEM((8, 512), F32),
            pltpu.SMEM((1,), jnp.int32),
            pltpu.SMEM((1,), jnp.int32),
            dma((len(PIECES),)),
            dma((4,)),
            dma((n,)),
            dma((n,)),
            dma((8,)),
            dma((8,)),
            dma((24,)),
            dma((24,)),
            dma((24,)),
            dma((24,)),
        ],
        compiler_params=pltpu.CompilerParams(
            collective_id=0, has_side_effects=True, vmem_limit_bytes=48 << 20
        ),
        name="outer_step",
    )(local_params.reshape(4, 2, 16, 32, 512), global_params, momentum, step_counts, alive)
    out, nm = pl.pallas_call(
        store,
        out_shape=(jax.ShapeDtypeStruct((4, 2, 16, 32, 512), F32), jax.ShapeDtypeStruct((32, 8192), F32)),
        in_specs=[pl.BlockSpec(memory_space=pltpu.VMEM)] * 2,
        out_specs=(hbm, hbm),
        scratch_shapes=[dma((9,))],
        compiler_params=pltpu.CompilerParams(vmem_limit_bytes=16 << 20),
        name="store",
    )(out, nm)
    return out.reshape(4096, 512), nm


def solution(mesh):
    in_specs = (
        P("worker", None, "fsdp"),
        P(("worker", "fsdp"), None),
        P(("worker", "fsdp"), None),
        P("worker"),
        P("worker"),
    )
    out_specs = (P(None, "fsdp"), P(("worker", "fsdp"), None))
    return jax.shard_map(local, mesh=mesh, in_specs=in_specs, out_specs=out_specs, check_vma=False)
```

```python
import functools

import jax
import jax.numpy as jnp
from jax import lax
from jax.experimental import pallas as pl
from jax.experimental.pallas import tpu as pltpu
from jax.sharding import PartitionSpec as P

MESH = pl.DeviceIdType.MESH
F32 = jnp.float32

A = ((0, 4, 0, 16), (4, 4, 0, 16), (8, 4, 0, 16), (12, 4, 0, 16), (0, 4, 16, 16),)
B = ((4, 4, 16, 16), (8, 4, 16, 16), (12, 4, 16, 16),)
ORDER = [(c[0], c[1], int(c[2])) for c in (
    "LA0", "H00", "LA1", "LA2", "LB0", "LA3", "CA0", "CA1", "LB1", "CA2", "ZA0", "CA3",
    "LB2", "ZA1", "LA4", "FB0", "FB1", "ZA2", "ZA3", "FB2", "CA4", "CB0", "CB1", "CB2",
    "NA0", "ZA4", "NA1", "NA2", "NA3", "GA0", "PA0", "NA4", "GA1", "NB0", "GA2", "NB1",
    "GA3", "U00", "XA0", "NB2", "GA4", "V00", "XA1", "GB0", "XA2", "XA3", "GB1", "XB0",
    "XA4", "YA0", "XB1", "GB2", "PA1", "PA2", "XB2", "PA3", "EA0", "YB0", "M00", "PA4",
    "YB1", "YA1", "YA2", "YB2", "YA3", "EB0", "YA4", "EA1", "EB1", "EA2", "EA3", "EB2",
    "EA4",
)]


PIECES = {(kind, p): piece for kind, sizes in (("A", A), ("B", B)) for p, piece in enumerate(sizes)}


def part(key):
    f, nf, r, nr = PIECES[key]
    rows = pl.ds(r, nr)
    return (pl.ds(f, nf), rows), (pl.ds(f, nf // 2), rows), (pl.ds(f + nf // 2, nf // 2), rows)


LAG = 24
TAGS = {
    "A": ("fr", "fl", "cr", "cl", "z", "gz", "gr", "gl", "pr", "pl", "xr", "xl", "yr", "yl"),
    "B": ("zb0", "zb1", "zb2", "zb3", "fr", "fl", "cr", "cl", "gr", "gl", "xr", "xl", "gz0", "gz1", "gz2", "gz3"),
}
INDEX = {key: i for i, key in enumerate((t, k, p) for (k, p) in PIECES for t in TAGS[k])}


def kernel(
    local_ref, g_hbm, m_hbm, steps_hbm, alive_hbm, out, nm_out,
    work, rf, rcl, rcr, rz, g, m, hs, hr, hp, avr, wt, inv, scale, steps_ref, alive_ref,
    load_sem, gm_sem, send_sem, recv_sem, wt_send, wt_recv, h_send, h_recv, v_send, v_recv,
):
    w, f = lax.axis_index("worker"), lax.axis_index("fsdp")
    y, zh = w // 2, w % 2
    zo = 1 - zh
    yr, yl, y2 = (y + 1) % 4, (y + 3) % 4, (y + 2) % 4
    zl, fl = f // 8, f % 8

    def across(d):
        return y * 2 + zo, (1 - zl) * 8 + (fl + d) % 8

    right, left, over = (yr * 2 + zh, f), (yl * 2 + zh, f), (y * 2 + zo, f)

    def load(key):
        rows = part(key)[0]
        i = list(PIECES).index(key)
        return pltpu.make_async_copy(local_ref.at[:, :, *rows], work.at[:, :, *rows], load_sem.at[i])

    lorder = [(k, p) for s, k, p in ORDER if s == "L"]
    for key in lorder[:2]:
        load(key).start()
    steps_copy = pltpu.make_async_copy(steps_hbm, steps_ref, gm_sem.at[2])
    alive_copy = pltpu.make_async_copy(alive_hbm, alive_ref, gm_sem.at[3])
    steps_copy.start()
    alive_copy.start()
    g_copy = pltpu.make_async_copy(g_hbm, g, gm_sem.at[0])
    m_copy = pltpu.make_async_copy(m_hbm, m, gm_sem.at[1])

    barrier = pltpu.get_barrier_semaphore()

    def greet_worker(d, c):
        pl.semaphore_signal(barrier, inc=1, device_id=((w + d) % 8, f), device_id_type=MESH)
        return c

    def greet_fsdp(d, c):
        pl.semaphore_signal(barrier, inc=1, device_id=(w, (f + d) % 16), device_id_type=MESH)
        return c

    def greet_across(d, c):
        pl.semaphore_signal(barrier, inc=1, device_id=across(d), device_id_type=MESH)
        return c

    lax.fori_loop(1, 8, greet_worker, 0)
    lax.fori_loop(1, 16, greet_fsdp, 0)
    lax.fori_loop(0, 8, greet_across, 0)
    g_copy.start()
    m_copy.start()
    for key in lorder[2:]:
        load(key).start()
    steps_copy.wait()
    alive_copy.wait()

    weight = (steps_ref[0] * alive_ref[0]).astype(F32)

    def channel(tag, kind, p):
        rows, lo, hi = part((kind, p))
        if tag[:2] == "zb":
            t = {"0": y, "1": yr, "2": y2, "3": yl}[tag[2]]
            return work.at[t, zo, *rows], rz.at[t, *rows], over, rz.at[t, *rows]
        if tag == "z":
            return work.at[y, zo, *rows], rz.at[0, *rows], over, rz.at[0, *rows]
        if tag in ("fr", "fl", "cr", "cl"):
            z, q = (slice(None), slice(None)) if kind == "A" else (zh, 0)
            if tag == "fr":
                return work.at[y2, z, *lo], rf.at[q, *lo], right, rf.at[q, *lo]
            if tag == "fl":
                return work.at[y2, z, *hi], rf.at[q, *hi], left, rf.at[q, *hi]
            if tag == "cr":
                return work.at[yr, z, *rows], rcl.at[q, *rows], right, rcl.at[q, *rows]
            return work.at[yl, z, *rows], rcr.at[q, *rows], left, rcr.at[q, *rows]
        if tag[:2] == "gz":
            t = {"": y, "0": y, "1": yl, "2": y2, "3": yr}[tag[2:]]
            return out.at[t, zh, *rows], out.at[t, zh, *rows], over, out.at[t, zo, *rows]
        z = zo if tag[0] in "py" else zh
        if tag in ("gr", "pr"):
            return out.at[y, z, *rows], out.at[y, z, *rows], right, out.at[yl, z, *rows]
        if tag in ("gl", "pl"):
            return out.at[y, z, *rows], out.at[y, z, *rows], left, out.at[yr, z, *rows]
        if tag in ("xr", "yr"):
            return out.at[yl, z, *lo], out.at[yl, z, *lo], right, out.at[y2, z, *lo]
        return out.at[yr, z, *hi], out.at[yr, z, *hi], left, out.at[y2, z, *hi]

    sent = []

    def send(tag, kind, p):
        src, dst, device, _ = channel(tag, kind, p)
        i = INDEX[tag, kind, p]
        copy = pltpu.make_async_remote_copy(
            src, dst, send_sem.at[i], recv_sem.at[i], device_id=device, device_id_type=MESH
        )
        copy.start()
        sent.append((now, copy))

    def wait(tag, kind, p):
        src, _, device, land = channel(tag, kind, p)
        i = INDEX[tag, kind, p]
        pltpu.make_async_remote_copy(
            src, land, send_sem.at[i], recv_sem.at[i], device_id=device, device_id_type=MESH
        ).wait_recv()

    def weigh(key):
        rows = part(key)[0]
        load(key).wait()

        def body(i, c):
            ref = work.at[i // 2, i % 2, *rows]
            ref[...] = ref[...] * weight
            return c

        lax.fori_loop(0, 8, body, 0)

    def wt_copy(d):
        to, source = (w + d) % 8, (w + 8 - d) % 8
        return pltpu.make_async_remote_copy(
            wt.at[w], wt.at[w], wt_send.at[d], wt_recv.at[d], device_id=(to, f), device_id_type=MESH
        ), pltpu.make_async_remote_copy(
            wt.at[w], wt.at[source], wt_send.at[d], wt_recv.at[d], device_id=(to, f), device_id_type=MESH
        )

    def near(d):
        return zl * 8 + (fl + d) % 8, zl * 8 + (fl + 8 - d) % 8

    def cross(d):
        return (1 - zl) * 8 + (fl + d) % 8, (1 - zl) * 8 + (fl + 8 - d) % 8

    def both(src, dst, land, send, recv, i, device):
        return tuple(
            pltpu.make_async_remote_copy(
                src, t, send.at[i], recv.at[i], device_id=device, device_id_type=MESH
            )
            for t in (dst, land)
        )

    first, last = pl.ds(0, 16), pl.ds(16, 16)

    def h_near(d):
        to, source = near(d)
        return both(hs.at[to], hr.at[f], hr.at[source], h_send, h_recv, d, (w, to))

    def h_cross(d):
        to, source = cross(d)
        return both(
            hs.at[to, last], hr.at[f, last], hr.at[source, last], h_send, h_recv, 8 + d, (w, to)
        )

    def h_over(d):
        to, source = cross(d)
        return both(hs.at[to, first], hp.at[f], hp.at[source], h_send, h_recv, 16 + d, across(d))

    def v_near(d):
        to, source = near(d)
        return both(out.at[y, zh, to], avr.at[f], avr.at[source], v_send, v_recv, d, (w, to))

    def v_cross(d):
        to, source = cross(d)
        return both(
            out.at[y, zh, to, last], avr.at[f, last], avr.at[source, last],
            v_send, v_recv, 8 + d, (w, to),
        )

    def v_over(d):
        to, source = cross(d)
        return both(
            out.at[y, zo, to, first], avr.at[f, first], avr.at[source, first],
            v_send, v_recv, 16 + d, across(d),
        )

    def each(copies, n, what, first=1):
        def body(d, c):
            out_copy, in_copy = copies(d)
            if what == "start":
                out_copy.start()
            elif what == "recv":
                in_copy.wait_recv()
            else:
                out_copy.wait_send()
            return c

        lax.fori_loop(first, n, body, 0)

    ready = []

    def need_h():
        if ready:
            return
        ready.append(True)
        each(wt_copy, 8, "recv")
        total = wt[0]
        for i in range(1, 8):
            total = total + wt[i]
        inv[...] = 1.33 / total
        scale[...] = total / 1.33
        each(h_near, 8, "recv")
        each(h_cross, 8, "recv", 0)
        each(h_over, 8, "recv", 0)

    def finish(rows, s):
        out[y, zh, *rows] = s * inv[0:1, :] + hr[*rows]

    entered = []
    for now, (step, kind, p) in enumerate(ORDER):
        while sent and sent[0][0] < now - LAG:
            sent.pop(0)[1].wait_send()
        if step == "H":
            g_copy.wait()
            m_copy.wait()
            for i in range(16):
                cols = pl.ds(512 * i, 512)
                hs[i] = -0.33 * g[:, cols] - 0.567 * m[:, cols]
            hr[f] = hs[f]
            hr[pl.ds((1 - zl) * 8, 8), first] = jnp.zeros((8, 16, 512), F32)
            hp[pl.ds(zl * 8, 8)] = jnp.zeros((8, 16, 512), F32)
            each(wt_copy, 8, "start")
            each(h_cross, 8, "start", 0)
            each(h_over, 8, "start", 0)
            each(h_near, 8, "start")
            continue
        if step == "V":
            avr[f] = out[y, zh, f]
            each(v_cross, 8, "start", 0)
            each(v_near, 8, "start")
            continue
        if step == "U":
            each(v_over, 8, "start", 0)
            continue
        if step == "M":
            each(v_near, 8, "recv")
            each(v_cross, 8, "recv", 0)
            each(v_over, 8, "recv", 0)
            each(wt_copy, 8, "sent")
            for copies in (h_near, v_near):
                each(copies, 8, "sent")
            for copies in (h_cross, h_over, v_cross, v_over):
                each(copies, 8, "sent", 0)
            for i in range(16):
                cols = pl.ds(512 * i, 512)
                average = (avr[i] + 0.33 * g[:, cols] + 0.567 * m[:, cols]) * (1 / 1.33)
                nm_out[:, cols] = 0.9 * m[:, cols] + (g[:, cols] - average)
            continue
        rows, lo, hi = part((kind, p))
        if step == "L":
            weigh((kind, p))
            if not entered:
                entered.append(True)
                wt[w] = jnp.full((8, 512), weight, F32)
                pl.semaphore_wait(barrier, 30)
            for tag in ("fr", "fl") if kind == "A" else ("zb2", "zb1", "zb3", "zb0"):
                send(tag, kind, p)
        elif step == "F":
            wait("zb2", kind, p)
            work[y2, zh, *rows] += rz[y2, *rows]
            send("fr", kind, p)
            send("fl", kind, p)
        elif step == "C":
            wait("fr", kind, p)
            wait("fl", kind, p)
            if kind == "A":
                for z in range(2):
                    work[yr, z, *lo] += rf[z, *lo]
                    work[yl, z, *hi] += rf[z, *hi]
            else:
                wait("zb1", kind, p)
                wait("zb3", kind, p)
                work[yr, zh, *lo] += rz[yr, *lo] + rf[0, *lo]
                work[yr, zh, *hi] += rz[yr, *hi]
                work[yl, zh, *lo] += rz[yl, *lo]
                work[yl, zh, *hi] += rz[yl, *hi] + rf[0, *hi]
            send("cr", kind, p)
            send("cl", kind, p)
        elif step == "Z":
            wait("cr", kind, p)
            wait("cl", kind, p)
            for z in range(2):
                work[y, z, *rows] += rcl[z, *rows] + rcr[z, *rows]
            fs, fn, r, _ = PIECES[kind, p]
            if r < 16:
                need_h()
                work[y, zo, *rows] += hp[fs : fs + fn] * scale[0:1, :]
            send("z", kind, p)
        elif step == "N":
            if kind == "A":
                wait("z", kind, p)
                need_h()
                finish(rows, work[y, zh, *rows] + rz[0, *rows])
                for tag in ("gz", "gr", "gl"):
                    send(tag, kind, p)
            else:
                wait("cr", kind, p)
                wait("cl", kind, p)
                wait("zb0", kind, p)
                need_h()
                finish(rows, work[y, zh, *rows] + rz[y, *rows] + rcl[0, *rows] + rcr[0, *rows])
                for tag in ("gr", "gl", "gz0"):
                    send(tag, kind, p)
        elif step == "P":
            send("pr", kind, p)
            send("pl", kind, p)
        elif step == "X":
            wait("gr", kind, p)
            wait("gl", kind, p)
            send("xr", kind, p)
            send("xl", kind, p)
            if kind == "B":
                send("gz1", kind, p)
                send("gz3", kind, p)
        elif step == "Y":
            if kind == "A":
                wait("pr", kind, p)
                wait("pl", kind, p)
                send("yr", kind, p)
                send("yl", kind, p)
            else:
                wait("xr", kind, p)
                wait("xl", kind, p)
                send("gz2", kind, p)
        elif step == "G":
            wait("gz0" if kind == "B" else "gz", kind, p)
        elif step == "E":
            for tag in ("xr", "xl", "yr", "yl") if kind == "A" else ("gz1", "gz3", "gz2"):
                wait(tag, kind, p)

    for _, copy in sent:
        copy.wait_send()


def store(a_ref, b_ref, a_out, b_out, sem):
    copies = [pltpu.make_async_copy(a_ref.at[i // 2, i % 2], a_out.at[i // 2, i % 2], sem.at[i]) for i in range(8)]
    copies.append(pltpu.make_async_copy(b_ref, b_out, sem.at[8]))
    for copy in copies:
        copy.start()
    for copy in copies:
        copy.wait()


def local(local_params, global_params, momentum, step_counts, alive):
    hbm = pl.BlockSpec(memory_space=pltpu.HBM)
    n = len(INDEX)
    dma = pltpu.SemaphoreType.DMA
    out, nm = pl.pallas_call(
        kernel,
        out_shape=(pltpu.VMEM((4, 2, 16, 32, 512), F32), pltpu.VMEM((32, 8192), F32)),
        in_specs=[hbm] * 5,
        out_specs=(pl.BlockSpec(memory_space=pltpu.VMEM), pl.BlockSpec(memory_space=pltpu.VMEM)),
        scratch_shapes=[
            pltpu.VMEM((4, 2, 16, 32, 512), F32),
            pltpu.VMEM((2, 16, 32, 512), F32),
            pltpu.VMEM((2, 16, 32, 512), F32),
            pltpu.VMEM((2, 16, 32, 512), F32),
            pltpu.VMEM((4, 16, 32, 512), F32),
            pltpu.VMEM((32, 8192), F32),
            pltpu.VMEM((32, 8192), F32),
            pltpu.VMEM((16, 32, 512), F32),
            pltpu.VMEM((16, 32, 512), F32),
            pltpu.VMEM((16, 16, 512), F32),
            pltpu.VMEM((16, 32, 512), F32),
            pltpu.VMEM((8, 8, 512), F32),
            pltpu.VMEM((8, 512), F32),
            pltpu.VMEM((8, 512), F32),
            pltpu.SMEM((1,), jnp.int32),
            pltpu.SMEM((1,), jnp.int32),
            dma((len(PIECES),)),
            dma((4,)),
            dma((n,)),
            dma((n,)),
            dma((8,)),
            dma((8,)),
            dma((24,)),
            dma((24,)),
            dma((24,)),
            dma((24,)),
        ],
        compiler_params=pltpu.CompilerParams(
            collective_id=0, has_side_effects=True, vmem_limit_bytes=48 << 20
        ),
        name="outer_step",
    )(local_params.reshape(4, 2, 16, 32, 512), global_params, momentum, step_counts, alive)
    out, nm = pl.pallas_call(
        store,
        out_shape=(jax.ShapeDtypeStruct((4, 2, 16, 32, 512), F32), jax.ShapeDtypeStruct((32, 8192), F32)),
        in_specs=[pl.BlockSpec(memory_space=pltpu.VMEM)] * 2,
        out_specs=(hbm, hbm),
        scratch_shapes=[dma((9,))],
        compiler_params=pltpu.CompilerParams(vmem_limit_bytes=16 << 20),
        name="store",
    )(out, nm)
    return out.reshape(4096, 512), nm


def solution(mesh):
    in_specs = (
        P("worker", None, "fsdp"),
        P(("worker", "fsdp"), None),
        P(("worker", "fsdp"), None),
        P("worker"),
        P("worker"),
    )
    out_specs = (P(None, "fsdp"), P(("worker", "fsdp"), None))
    return jax.shard_map(local, mesh=mesh, in_specs=in_specs, out_specs=out_specs, check_vma=False)
```

```python
import functools

import jax
import jax.numpy as jnp
from jax import lax
from jax.experimental import pallas as pl
from jax.experimental.pallas import tpu as pltpu
from jax.sharding import PartitionSpec as P

MESH = pl.DeviceIdType.MESH
F32 = jnp.float32

A = ((0, 8, 0, 16), (8, 8, 0, 16), (0, 4, 16, 16),)
B = ((4, 4, 16, 16), (8, 8, 16, 16),)
ORDER = [(c[0], c[1], int(c[2])) for c in (
    "LA0", "LA1", "H00", "LA2", "LB0", "CA0", "LB1", "FB0", "CA1", "ZA0", "FB1", "CB0",
    "CA2", "ZA1", "CB1", "NA0", "ZA2", "NA1", "GA0", "PA0", "NA2", "GA1", "U00", "NB0",
    "GA2", "NB1", "V00", "GB0", "YA0", "XB0", "XA0", "GB1", "XA1", "XB1", "XA2", "PA1",
    "EA0", "M00", "YB0", "PA2", "YB1", "YA1", "EB0", "YA2", "EA1", "EB1", "EA2",
)]


PIECES = {(kind, p): piece for kind, sizes in (("A", A), ("B", B)) for p, piece in enumerate(sizes)}


def part(key):
    f, nf, r, nr = PIECES[key]
    rows = pl.ds(r, nr)
    return (pl.ds(f, nf), rows), (pl.ds(f, nf // 2), rows), (pl.ds(f + nf // 2, nf // 2), rows)


LAG = 24
TAGS = {
    "A": ("fr", "fl", "cr", "cl", "z", "gz", "gr", "gl", "pr", "pl", "xr", "xl", "yr", "yl"),
    "B": ("zb0", "zb1", "zb2", "zb3", "fr", "fl", "cr", "cl", "gr", "gl", "xr", "xl", "gz0", "gz1", "gz2", "gz3"),
}
INDEX = {key: i for i, key in enumerate((t, k, p) for (k, p) in PIECES for t in TAGS[k])}


def kernel(
    local_ref, g_hbm, m_hbm, steps_hbm, alive_hbm, out, nm_out,
    work, rf, rcl, rcr, rz, g, m, hs, hr, hp, avr, wt, inv, scale, steps_ref, alive_ref,
    load_sem, gm_sem, send_sem, recv_sem, wt_send, wt_recv, h_send, h_recv, v_send, v_recv,
):
    w, f = lax.axis_index("worker"), lax.axis_index("fsdp")
    y, zh = w // 2, w % 2
    zo = 1 - zh
    yr, yl, y2 = (y + 1) % 4, (y + 3) % 4, (y + 2) % 4
    zl, fl = f // 8, f % 8

    def across(d):
        return y * 2 + zo, (1 - zl) * 8 + (fl + d) % 8

    right, left, over = (yr * 2 + zh, f), (yl * 2 + zh, f), (y * 2 + zo, f)

    def load(key):
        rows = part(key)[0]
        i = list(PIECES).index(key)
        return pltpu.make_async_copy(local_ref.at[:, :, *rows], work.at[:, :, *rows], load_sem.at[i])

    lorder = [(k, p) for s, k, p in ORDER if s == "L"]
    for key in lorder[:2]:
        load(key).start()
    steps_copy = pltpu.make_async_copy(steps_hbm, steps_ref, gm_sem.at[2])
    alive_copy = pltpu.make_async_copy(alive_hbm, alive_ref, gm_sem.at[3])
    steps_copy.start()
    alive_copy.start()
    g_copy = pltpu.make_async_copy(g_hbm, g, gm_sem.at[0])
    m_copy = pltpu.make_async_copy(m_hbm, m, gm_sem.at[1])

    barrier = pltpu.get_barrier_semaphore()

    def greet_worker(d, c):
        pl.semaphore_signal(barrier, inc=1, device_id=((w + d) % 8, f), device_id_type=MESH)
        return c

    def greet_fsdp(d, c):
        pl.semaphore_signal(barrier, inc=1, device_id=(w, (f + d) % 16), device_id_type=MESH)
        return c

    def greet_across(d, c):
        pl.semaphore_signal(barrier, inc=1, device_id=across(d), device_id_type=MESH)
        return c

    lax.fori_loop(1, 8, greet_worker, 0)
    lax.fori_loop(1, 16, greet_fsdp, 0)
    lax.fori_loop(0, 8, greet_across, 0)
    g_copy.start()
    m_copy.start()
    for key in lorder[2:]:
        load(key).start()
    steps_copy.wait()
    alive_copy.wait()

    weight = (steps_ref[0] * alive_ref[0]).astype(F32)

    def channel(tag, kind, p):
        rows, lo, hi = part((kind, p))
        if tag[:2] == "zb":
            t = {"0": y, "1": yr, "2": y2, "3": yl}[tag[2]]
            return work.at[t, zo, *rows], rz.at[t, *rows], over, rz.at[t, *rows]
        if tag == "z":
            return work.at[y, zo, *rows], rz.at[0, *rows], over, rz.at[0, *rows]
        if tag in ("fr", "fl", "cr", "cl"):
            z, q = (slice(None), slice(None)) if kind == "A" else (zh, 0)
            if tag == "fr":
                return work.at[y2, z, *lo], rf.at[q, *lo], right, rf.at[q, *lo]
            if tag == "fl":
                return work.at[y2, z, *hi], rf.at[q, *hi], left, rf.at[q, *hi]
            if tag == "cr":
                return work.at[yr, z, *rows], rcl.at[q, *rows], right, rcl.at[q, *rows]
            return work.at[yl, z, *rows], rcr.at[q, *rows], left, rcr.at[q, *rows]
        if tag[:2] == "gz":
            t = {"": y, "0": y, "1": yl, "2": y2, "3": yr}[tag[2:]]
            return out.at[t, zh, *rows], out.at[t, zh, *rows], over, out.at[t, zo, *rows]
        z = zo if tag[0] in "py" else zh
        if tag in ("gr", "pr"):
            return out.at[y, z, *rows], out.at[y, z, *rows], right, out.at[yl, z, *rows]
        if tag in ("gl", "pl"):
            return out.at[y, z, *rows], out.at[y, z, *rows], left, out.at[yr, z, *rows]
        if tag in ("xr", "yr"):
            return out.at[yl, z, *lo], out.at[yl, z, *lo], right, out.at[y2, z, *lo]
        return out.at[yr, z, *hi], out.at[yr, z, *hi], left, out.at[y2, z, *hi]

    sent = []

    def send(tag, kind, p):
        src, dst, device, _ = channel(tag, kind, p)
        i = INDEX[tag, kind, p]
        copy = pltpu.make_async_remote_copy(
            src, dst, send_sem.at[i], recv_sem.at[i], device_id=device, device_id_type=MESH
        )
        copy.start()
        sent.append((now, copy))

    def wait(tag, kind, p):
        src, _, device, land = channel(tag, kind, p)
        i = INDEX[tag, kind, p]
        pltpu.make_async_remote_copy(
            src, land, send_sem.at[i], recv_sem.at[i], device_id=device, device_id_type=MESH
        ).wait_recv()

    def weigh(key):
        rows = part(key)[0]
        load(key).wait()

        def body(i, c):
            ref = work.at[i // 2, i % 2, *rows]
            ref[...] = ref[...] * weight
            return c

        lax.fori_loop(0, 8, body, 0)

    def wt_copy(d):
        to, source = (w + d) % 8, (w + 8 - d) % 8
        return pltpu.make_async_remote_copy(
            wt.at[w], wt.at[w], wt_send.at[d], wt_recv.at[d], device_id=(to, f), device_id_type=MESH
        ), pltpu.make_async_remote_copy(
            wt.at[w], wt.at[source], wt_send.at[d], wt_recv.at[d], device_id=(to, f), device_id_type=MESH
        )

    def near(d):
        return zl * 8 + (fl + d) % 8, zl * 8 + (fl + 8 - d) % 8

    def cross(d):
        return (1 - zl) * 8 + (fl + d) % 8, (1 - zl) * 8 + (fl + 8 - d) % 8

    def both(src, dst, land, send, recv, i, device):
        return tuple(
            pltpu.make_async_remote_copy(
                src, t, send.at[i], recv.at[i], device_id=device, device_id_type=MESH
            )
            for t in (dst, land)
        )

    first, last = pl.ds(0, 16), pl.ds(16, 16)

    def h_near(d):
        to, source = near(d)
        return both(hs.at[to], hr.at[f], hr.at[source], h_send, h_recv, d, (w, to))

    def h_cross(d):
        to, source = cross(d)
        return both(
            hs.at[to, last], hr.at[f, last], hr.at[source, last], h_send, h_recv, 8 + d, (w, to)
        )

    def h_over(d):
        to, source = cross(d)
        return both(hs.at[to, first], hp.at[f], hp.at[source], h_send, h_recv, 16 + d, across(d))

    def v_near(d):
        to, source = near(d)
        return both(out.at[y, zh, to], avr.at[f], avr.at[source], v_send, v_recv, d, (w, to))

    def v_cross(d):
        to, source = cross(d)
        return both(
            out.at[y, zh, to, last], avr.at[f, last], avr.at[source, last],
            v_send, v_recv, 8 + d, (w, to),
        )

    def v_over(d):
        to, source = cross(d)
        return both(
            out.at[y, zo, to, first], avr.at[f, first], avr.at[source, first],
            v_send, v_recv, 16 + d, across(d),
        )

    def each(copies, n, what, first=1):
        def body(d, c):
            out_copy, in_copy = copies(d)
            if what == "start":
                out_copy.start()
            elif what == "recv":
                in_copy.wait_recv()
            else:
                out_copy.wait_send()
            return c

        lax.fori_loop(first, n, body, 0)

    ready = []

    def need_h():
        if ready:
            return
        ready.append(True)
        each(wt_copy, 8, "recv")
        total = wt[0]
        for i in range(1, 8):
            total = total + wt[i]
        inv[...] = 1.33 / total
        scale[...] = total / 1.33
        each(h_near, 8, "recv")
        each(h_cross, 8, "recv", 0)
        each(h_over, 8, "recv", 0)

    def finish(rows, s):
        out[y, zh, *rows] = s * inv[0:1, :] + hr[*rows]

    entered = []
    for now, (step, kind, p) in enumerate(ORDER):
        while sent and sent[0][0] < now - LAG:
            sent.pop(0)[1].wait_send()
        if step == "H":
            g_copy.wait()
            m_copy.wait()
            for i in range(16):
                cols = pl.ds(512 * i, 512)
                hs[i] = -0.33 * g[:, cols] - 0.567 * m[:, cols]
            hr[f] = hs[f]
            hr[pl.ds((1 - zl) * 8, 8), first] = jnp.zeros((8, 16, 512), F32)
            hp[pl.ds(zl * 8, 8)] = jnp.zeros((8, 16, 512), F32)
            each(wt_copy, 8, "start")
            each(h_cross, 8, "start", 0)
            each(h_over, 8, "start", 0)
            each(h_near, 8, "start")
            continue
        if step == "V":
            avr[f] = out[y, zh, f]
            each(v_cross, 8, "start", 0)
            each(v_near, 8, "start")
            continue
        if step == "U":
            each(v_over, 8, "start", 0)
            continue
        if step == "M":
            each(v_near, 8, "recv")
            each(v_cross, 8, "recv", 0)
            each(v_over, 8, "recv", 0)
            each(wt_copy, 8, "sent")
            for copies in (h_near, v_near):
                each(copies, 8, "sent")
            for copies in (h_cross, h_over, v_cross, v_over):
                each(copies, 8, "sent", 0)
            for i in range(16):
                cols = pl.ds(512 * i, 512)
                average = (avr[i] + 0.33 * g[:, cols] + 0.567 * m[:, cols]) * (1 / 1.33)
                nm_out[:, cols] = 0.9 * m[:, cols] + (g[:, cols] - average)
            continue
        rows, lo, hi = part((kind, p))
        if step == "L":
            weigh((kind, p))
            if not entered:
                entered.append(True)
                wt[w] = jnp.full((8, 512), weight, F32)
                pl.semaphore_wait(barrier, 30)
            for tag in ("fr", "fl") if kind == "A" else ("zb2", "zb1", "zb3", "zb0"):
                send(tag, kind, p)
        elif step == "F":
            wait("zb2", kind, p)
            work[y2, zh, *rows] += rz[y2, *rows]
            send("fr", kind, p)
            send("fl", kind, p)
        elif step == "C":
            wait("fr", kind, p)
            wait("fl", kind, p)
            if kind == "A":
                for z in range(2):
                    work[yr, z, *lo] += rf[z, *lo]
                    work[yl, z, *hi] += rf[z, *hi]
            else:
                wait("zb1", kind, p)
                wait("zb3", kind, p)
                work[yr, zh, *lo] += rz[yr, *lo] + rf[0, *lo]
                work[yr, zh, *hi] += rz[yr, *hi]
                work[yl, zh, *lo] += rz[yl, *lo]
                work[yl, zh, *hi] += rz[yl, *hi] + rf[0, *hi]
            send("cr", kind, p)
            send("cl", kind, p)
        elif step == "Z":
            wait("cr", kind, p)
            wait("cl", kind, p)
            for z in range(2):
                work[y, z, *rows] += rcl[z, *rows] + rcr[z, *rows]
            fs, fn, r, _ = PIECES[kind, p]
            if r < 16:
                need_h()
                work[y, zo, *rows] += hp[fs : fs + fn] * scale[0:1, :]
            send("z", kind, p)
        elif step == "N":
            if kind == "A":
                wait("z", kind, p)
                need_h()
                finish(rows, work[y, zh, *rows] + rz[0, *rows])
                for tag in ("gz", "gr", "gl"):
                    send(tag, kind, p)
            else:
                wait("cr", kind, p)
                wait("cl", kind, p)
                wait("zb0", kind, p)
                need_h()
                finish(rows, work[y, zh, *rows] + rz[y, *rows] + rcl[0, *rows] + rcr[0, *rows])
                for tag in ("gr", "gl", "gz0"):
                    send(tag, kind, p)
        elif step == "P":
            send("pr", kind, p)
            send("pl", kind, p)
        elif step == "X":
            wait("gr", kind, p)
            wait("gl", kind, p)
            send("xr", kind, p)
            send("xl", kind, p)
            if kind == "B":
                send("gz1", kind, p)
                send("gz3", kind, p)
        elif step == "Y":
            if kind == "A":
                wait("pr", kind, p)
                wait("pl", kind, p)
                send("yr", kind, p)
                send("yl", kind, p)
            else:
                wait("xr", kind, p)
                wait("xl", kind, p)
                send("gz2", kind, p)
        elif step == "G":
            wait("gz0" if kind == "B" else "gz", kind, p)
        elif step == "E":
            for tag in ("xr", "xl", "yr", "yl") if kind == "A" else ("gz1", "gz3", "gz2"):
                wait(tag, kind, p)

    for _, copy in sent:
        copy.wait_send()


def store(a_ref, b_ref, a_out, b_out, sem):
    copies = [pltpu.make_async_copy(a_ref.at[i // 2, i % 2], a_out.at[i // 2, i % 2], sem.at[i]) for i in range(8)]
    copies.append(pltpu.make_async_copy(b_ref, b_out, sem.at[8]))
    for copy in copies:
        copy.start()
    for copy in copies:
        copy.wait()


def local(local_params, global_params, momentum, step_counts, alive):
    hbm = pl.BlockSpec(memory_space=pltpu.HBM)
    n = len(INDEX)
    dma = pltpu.SemaphoreType.DMA
    out, nm = pl.pallas_call(
        kernel,
        out_shape=(pltpu.VMEM((4, 2, 16, 32, 512), F32), pltpu.VMEM((32, 8192), F32)),
        in_specs=[hbm] * 5,
        out_specs=(pl.BlockSpec(memory_space=pltpu.VMEM), pl.BlockSpec(memory_space=pltpu.VMEM)),
        scratch_shapes=[
            pltpu.VMEM((4, 2, 16, 32, 512), F32),
            pltpu.VMEM((2, 16, 32, 512), F32),
            pltpu.VMEM((2, 16, 32, 512), F32),
            pltpu.VMEM((2, 16, 32, 512), F32),
            pltpu.VMEM((4, 16, 32, 512), F32),
            pltpu.VMEM((32, 8192), F32),
            pltpu.VMEM((32, 8192), F32),
            pltpu.VMEM((16, 32, 512), F32),
            pltpu.VMEM((16, 32, 512), F32),
            pltpu.VMEM((16, 16, 512), F32),
            pltpu.VMEM((16, 32, 512), F32),
            pltpu.VMEM((8, 8, 512), F32),
            pltpu.VMEM((8, 512), F32),
            pltpu.VMEM((8, 512), F32),
            pltpu.SMEM((1,), jnp.int32),
            pltpu.SMEM((1,), jnp.int32),
            dma((len(PIECES),)),
            dma((4,)),
            dma((n,)),
            dma((n,)),
            dma((8,)),
            dma((8,)),
            dma((24,)),
            dma((24,)),
            dma((24,)),
            dma((24,)),
        ],
        compiler_params=pltpu.CompilerParams(
            collective_id=0, has_side_effects=True, vmem_limit_bytes=48 << 20
        ),
        name="outer_step",
    )(local_params.reshape(4, 2, 16, 32, 512), global_params, momentum, step_counts, alive)
    out, nm = pl.pallas_call(
        store,
        out_shape=(jax.ShapeDtypeStruct((4, 2, 16, 32, 512), F32), jax.ShapeDtypeStruct((32, 8192), F32)),
        in_specs=[pl.BlockSpec(memory_space=pltpu.VMEM)] * 2,
        out_specs=(hbm, hbm),
        scratch_shapes=[dma((9,))],
        compiler_params=pltpu.CompilerParams(vmem_limit_bytes=16 << 20),
        name="store",
    )(out, nm)
    return out.reshape(4096, 512), nm


def solution(mesh):
    in_specs = (
        P("worker", None, "fsdp"),
        P(("worker", "fsdp"), None),
        P(("worker", "fsdp"), None),
        P("worker"),
        P("worker"),
    )
    out_specs = (P(None, "fsdp"), P(("worker", "fsdp"), None))
    return jax.shard_map(local, mesh=mesh, in_specs=in_specs, out_specs=out_specs, check_vma=False)
```

```python
import functools

import jax
import jax.numpy as jnp
from jax import lax
from jax.experimental import pallas as pl
from jax.experimental.pallas import tpu as pltpu
from jax.sharding import PartitionSpec as P

MESH = pl.DeviceIdType.MESH
F32 = jnp.float32

A = ((0, 8, 0, 16), (8, 8, 0, 16), (0, 4, 16, 16),)
B = ((4, 4, 16, 16), (8, 8, 16, 16),)
ORDER = [(c[0], c[1], int(c[2])) for c in (
    "LA0", "LA1", "H00", "LA2", "LB0", "CA0", "LB1", "FB0", "CA1", "ZA0", "FB1", "CB0",
    "CA2", "ZA1", "CB1", "NB0", "ZA2", "NA0", "GB0", "NB1", "NA1", "GA0", "XA0", "GB1",
    "NA2", "V00", "PA0", "GA1", "U00", "GA2", "XB0", "XA1", "XB1", "XA2", "YA0", "PA1",
    "M00", "YB0", "PA2", "YB1", "EA0", "YA1", "EB0", "YA2", "EA1", "EB1", "EA2",
)]


PIECES = {(kind, p): piece for kind, sizes in (("A", A), ("B", B)) for p, piece in enumerate(sizes)}


def part(key):
    f, nf, r, nr = PIECES[key]
    rows = pl.ds(r, nr)
    return (pl.ds(f, nf), rows), (pl.ds(f, nf // 2), rows), (pl.ds(f + nf // 2, nf // 2), rows)


LAG = 24
TAGS = {
    "A": ("fr", "fl", "cr", "cl", "z", "gz", "gr", "gl", "pr", "pl", "xr", "xl", "yr", "yl"),
    "B": ("zb0", "zb1", "zb2", "zb3", "fr", "fl", "cr", "cl", "gr", "gl", "xr", "xl", "gz0", "gz1", "gz2", "gz3"),
}
INDEX = {key: i for i, key in enumerate((t, k, p) for (k, p) in PIECES for t in TAGS[k])}


def kernel(
    local_ref, g_hbm, m_hbm, steps_hbm, alive_hbm, out, nm_out,
    work, rf, rcl, rcr, rz, g, m, hs, hr, hp, avr, wt, inv, scale, steps_ref, alive_ref,
    load_sem, gm_sem, send_sem, recv_sem, wt_send, wt_recv, h_send, h_recv, v_send, v_recv,
):
    w, f = lax.axis_index("worker"), lax.axis_index("fsdp")
    y, zh = w // 2, w % 2
    zo = 1 - zh
    yr, yl, y2 = (y + 1) % 4, (y + 3) % 4, (y + 2) % 4
    zl, fl = f // 8, f % 8

    def across(d):
        return y * 2 + zo, (1 - zl) * 8 + (fl + d) % 8

    right, left, over = (yr * 2 + zh, f), (yl * 2 + zh, f), (y * 2 + zo, f)

    def load(key):
        rows = part(key)[0]
        i = list(PIECES).index(key)
        return pltpu.make_async_copy(local_ref.at[:, :, *rows], work.at[:, :, *rows], load_sem.at[i])

    lorder = [(k, p) for s, k, p in ORDER if s == "L"]
    for key in lorder[:2]:
        load(key).start()
    steps_copy = pltpu.make_async_copy(steps_hbm, steps_ref, gm_sem.at[2])
    alive_copy = pltpu.make_async_copy(alive_hbm, alive_ref, gm_sem.at[3])
    steps_copy.start()
    alive_copy.start()
    g_copy = pltpu.make_async_copy(g_hbm, g, gm_sem.at[0])
    m_copy = pltpu.make_async_copy(m_hbm, m, gm_sem.at[1])

    barrier = pltpu.get_barrier_semaphore()

    def greet_worker(d, c):
        pl.semaphore_signal(barrier, inc=1, device_id=((w + d) % 8, f), device_id_type=MESH)
        return c

    def greet_fsdp(d, c):
        pl.semaphore_signal(barrier, inc=1, device_id=(w, (f + d) % 16), device_id_type=MESH)
        return c

    def greet_across(d, c):
        pl.semaphore_signal(barrier, inc=1, device_id=across(d), device_id_type=MESH)
        return c

    lax.fori_loop(1, 8, greet_worker, 0)
    lax.fori_loop(1, 16, greet_fsdp, 0)
    lax.fori_loop(0, 8, greet_across, 0)
    g_copy.start()
    m_copy.start()
    for key in lorder[2:]:
        load(key).start()
    steps_copy.wait()
    alive_copy.wait()

    weight = (steps_ref[0] * alive_ref[0]).astype(F32)

    def channel(tag, kind, p):
        rows, lo, hi = part((kind, p))
        if tag[:2] == "zb":
            t = {"0": y, "1": yr, "2": y2, "3": yl}[tag[2]]
            return work.at[t, zo, *rows], rz.at[t, *rows], over, rz.at[t, *rows]
        if tag == "z":
            return work.at[y, zo, *rows], rz.at[0, *rows], over, rz.at[0, *rows]
        if tag in ("fr", "fl", "cr", "cl"):
            z, q = (slice(None), slice(None)) if kind == "A" else (zh, 0)
            if tag == "fr":
                return work.at[y2, z, *lo], rf.at[q, *lo], right, rf.at[q, *lo]
            if tag == "fl":
                return work.at[y2, z, *hi], rf.at[q, *hi], left, rf.at[q, *hi]
            if tag == "cr":
                return work.at[yr, z, *rows], rcl.at[q, *rows], right, rcl.at[q, *rows]
            return work.at[yl, z, *rows], rcr.at[q, *rows], left, rcr.at[q, *rows]
        if tag[:2] == "gz":
            t = {"": y, "0": y, "1": yl, "2": y2, "3": yr}[tag[2:]]
            return out.at[t, zh, *rows], out.at[t, zh, *rows], over, out.at[t, zo, *rows]
        z = zo if tag[0] in "py" else zh
        if tag in ("gr", "pr"):
            return out.at[y, z, *rows], out.at[y, z, *rows], right, out.at[yl, z, *rows]
        if tag in ("gl", "pl"):
            return out.at[y, z, *rows], out.at[y, z, *rows], left, out.at[yr, z, *rows]
        if tag in ("xr", "yr"):
            return out.at[yl, z, *lo], out.at[yl, z, *lo], right, out.at[y2, z, *lo]
        return out.at[yr, z, *hi], out.at[yr, z, *hi], left, out.at[y2, z, *hi]

    sent = []

    def send(tag, kind, p):
        src, dst, device, _ = channel(tag, kind, p)
        i = INDEX[tag, kind, p]
        copy = pltpu.make_async_remote_copy(
            src, dst, send_sem.at[i], recv_sem.at[i], device_id=device, device_id_type=MESH
        )
        copy.start()
        sent.append((now, copy))

    def wait(tag, kind, p):
        src, _, device, land = channel(tag, kind, p)
        i = INDEX[tag, kind, p]
        pltpu.make_async_remote_copy(
            src, land, send_sem.at[i], recv_sem.at[i], device_id=device, device_id_type=MESH
        ).wait_recv()

    def weigh(key):
        rows = part(key)[0]
        load(key).wait()

        def body(i, c):
            ref = work.at[i // 2, i % 2, *rows]
            ref[...] = ref[...] * weight
            return c

        lax.fori_loop(0, 8, body, 0)

    def wt_copy(d):
        to, source = (w + d) % 8, (w + 8 - d) % 8
        return pltpu.make_async_remote_copy(
            wt.at[w], wt.at[w], wt_send.at[d], wt_recv.at[d], device_id=(to, f), device_id_type=MESH
        ), pltpu.make_async_remote_copy(
            wt.at[w], wt.at[source], wt_send.at[d], wt_recv.at[d], device_id=(to, f), device_id_type=MESH
        )

    def near(d):
        return zl * 8 + (fl + d) % 8, zl * 8 + (fl + 8 - d) % 8

    def cross(d):
        return (1 - zl) * 8 + (fl + d) % 8, (1 - zl) * 8 + (fl + 8 - d) % 8

    def both(src, dst, land, send, recv, i, device):
        return tuple(
            pltpu.make_async_remote_copy(
                src, t, send.at[i], recv.at[i], device_id=device, device_id_type=MESH
            )
            for t in (dst, land)
        )

    first, last = pl.ds(0, 16), pl.ds(16, 16)

    def h_near(d):
        to, source = near(d)
        return both(hs.at[to], hr.at[f], hr.at[source], h_send, h_recv, d, (w, to))

    def h_cross(d):
        to, source = cross(d)
        return both(
            hs.at[to, last], hr.at[f, last], hr.at[source, last], h_send, h_recv, 8 + d, (w, to)
        )

    def h_over(d):
        to, source = cross(d)
        return both(hs.at[to, first], hp.at[f], hp.at[source], h_send, h_recv, 16 + d, across(d))

    def v_near(d):
        to, source = near(d)
        return both(out.at[y, zh, to], avr.at[f], avr.at[source], v_send, v_recv, d, (w, to))

    def v_cross(d):
        to, source = cross(d)
        return both(
            out.at[y, zh, to, last], avr.at[f, last], avr.at[source, last],
            v_send, v_recv, 8 + d, (w, to),
        )

    def v_over(d):
        to, source = cross(d)
        return both(
            out.at[y, zo, to, first], avr.at[f, first], avr.at[source, first],
            v_send, v_recv, 16 + d, across(d),
        )

    def each(copies, n, what, first=1):
        def body(d, c):
            out_copy, in_copy = copies(d)
            if what == "start":
                out_copy.start()
            elif what == "recv":
                in_copy.wait_recv()
            else:
                out_copy.wait_send()
            return c

        lax.fori_loop(first, n, body, 0)

    ready = []

    def need_h():
        if ready:
            return
        ready.append(True)
        each(wt_copy, 8, "recv")
        total = wt[0]
        for i in range(1, 8):
            total = total + wt[i]
        inv[...] = 1.33 / total
        scale[...] = total / 1.33
        each(h_near, 8, "recv")
        each(h_cross, 8, "recv", 0)
        each(h_over, 8, "recv", 0)

    def finish(rows, s):
        out[y, zh, *rows] = s * inv[0:1, :] + hr[*rows]

    entered = []
    for now, (step, kind, p) in enumerate(ORDER):
        while sent and sent[0][0] < now - LAG:
            sent.pop(0)[1].wait_send()
        if step == "H":
            g_copy.wait()
            m_copy.wait()
            for i in range(16):
                cols = pl.ds(512 * i, 512)
                hs[i] = -0.33 * g[:, cols] - 0.567 * m[:, cols]
            hr[f] = hs[f]
            hr[pl.ds((1 - zl) * 8, 8), first] = jnp.zeros((8, 16, 512), F32)
            hp[pl.ds(zl * 8, 8)] = jnp.zeros((8, 16, 512), F32)
            each(wt_copy, 8, "start")
            each(h_cross, 8, "start", 0)
            each(h_over, 8, "start", 0)
            each(h_near, 8, "start")
            continue
        if step == "V":
            avr[f] = out[y, zh, f]
            each(v_cross, 8, "start", 0)
            each(v_near, 8, "start")
            continue
        if step == "U":
            each(v_over, 8, "start", 0)
            continue
        if step == "M":
            each(v_near, 8, "recv")
            each(v_cross, 8, "recv", 0)
            each(v_over, 8, "recv", 0)
            each(wt_copy, 8, "sent")
            for copies in (h_near, v_near):
                each(copies, 8, "sent")
            for copies in (h_cross, h_over, v_cross, v_over):
                each(copies, 8, "sent", 0)
            for i in range(16):
                cols = pl.ds(512 * i, 512)
                average = (avr[i] + 0.33 * g[:, cols] + 0.567 * m[:, cols]) * (1 / 1.33)
                nm_out[:, cols] = 0.9 * m[:, cols] + (g[:, cols] - average)
            continue
        rows, lo, hi = part((kind, p))
        if step == "L":
            weigh((kind, p))
            if not entered:
                entered.append(True)
                wt[w] = jnp.full((8, 512), weight, F32)
                pl.semaphore_wait(barrier, 30)
            for tag in ("fr", "fl") if kind == "A" else ("zb2", "zb1", "zb3", "zb0"):
                send(tag, kind, p)
        elif step == "F":
            wait("zb2", kind, p)
            work[y2, zh, *rows] += rz[y2, *rows]
            send("fr", kind, p)
            send("fl", kind, p)
        elif step == "C":
            wait("fr", kind, p)
            wait("fl", kind, p)
            if kind == "A":
                for z in range(2):
                    work[yr, z, *lo] += rf[z, *lo]
                    work[yl, z, *hi] += rf[z, *hi]
            else:
                wait("zb1", kind, p)
                wait("zb3", kind, p)
                work[yr, zh, *lo] += rz[yr, *lo] + rf[0, *lo]
                work[yr, zh, *hi] += rz[yr, *hi]
                work[yl, zh, *lo] += rz[yl, *lo]
                work[yl, zh, *hi] += rz[yl, *hi] + rf[0, *hi]
            send("cr", kind, p)
            send("cl", kind, p)
        elif step == "Z":
            wait("cr", kind, p)
            wait("cl", kind, p)
            for z in range(2):
                work[y, z, *rows] += rcl[z, *rows] + rcr[z, *rows]
            fs, fn, r, _ = PIECES[kind, p]
            if r < 16:
                need_h()
                work[y, zo, *rows] += hp[fs : fs + fn] * scale[0:1, :]
            send("z", kind, p)
        elif step == "N":
            if kind == "A":
                wait("z", kind, p)
                need_h()
                finish(rows, work[y, zh, *rows] + rz[0, *rows])
                for tag in ("gz", "gr", "gl"):
                    send(tag, kind, p)
            else:
                wait("cr", kind, p)
                wait("cl", kind, p)
                wait("zb0", kind, p)
                need_h()
                finish(rows, work[y, zh, *rows] + rz[y, *rows] + rcl[0, *rows] + rcr[0, *rows])
                for tag in ("gr", "gl", "gz0"):
                    send(tag, kind, p)
        elif step == "P":
            send("pr", kind, p)
            send("pl", kind, p)
        elif step == "X":
            wait("gr", kind, p)
            wait("gl", kind, p)
            send("xr", kind, p)
            send("xl", kind, p)
            if kind == "B":
                send("gz1", kind, p)
                send("gz3", kind, p)
        elif step == "Y":
            if kind == "A":
                wait("pr", kind, p)
                wait("pl", kind, p)
                send("yr", kind, p)
                send("yl", kind, p)
            else:
                wait("xr", kind, p)
                wait("xl", kind, p)
                send("gz2", kind, p)
        elif step == "G":
            wait("gz0" if kind == "B" else "gz", kind, p)
        elif step == "E":
            for tag in ("xr", "xl", "yr", "yl") if kind == "A" else ("gz1", "gz3", "gz2"):
                wait(tag, kind, p)

    for _, copy in sent:
        copy.wait_send()


def store(a_ref, b_ref, a_out, b_out, sem):
    copies = [pltpu.make_async_copy(a_ref.at[i // 2, i % 2], a_out.at[i // 2, i % 2], sem.at[i]) for i in range(8)]
    copies.append(pltpu.make_async_copy(b_ref, b_out, sem.at[8]))
    for copy in copies:
        copy.start()
    for copy in copies:
        copy.wait()


def local(local_params, global_params, momentum, step_counts, alive):
    hbm = pl.BlockSpec(memory_space=pltpu.HBM)
    n = len(INDEX)
    dma = pltpu.SemaphoreType.DMA
    out, nm = pl.pallas_call(
        kernel,
        out_shape=(pltpu.VMEM((4, 2, 16, 32, 512), F32), pltpu.VMEM((32, 8192), F32)),
        in_specs=[hbm] * 5,
        out_specs=(pl.BlockSpec(memory_space=pltpu.VMEM), pl.BlockSpec(memory_space=pltpu.VMEM)),
        scratch_shapes=[
            pltpu.VMEM((4, 2, 16, 32, 512), F32),
            pltpu.VMEM((2, 16, 32, 512), F32),
            pltpu.VMEM((2, 16, 32, 512), F32),
            pltpu.VMEM((2, 16, 32, 512), F32),
            pltpu.VMEM((4, 16, 32, 512), F32),
            pltpu.VMEM((32, 8192), F32),
            pltpu.VMEM((32, 8192), F32),
            pltpu.VMEM((16, 32, 512), F32),
            pltpu.VMEM((16, 32, 512), F32),
            pltpu.VMEM((16, 16, 512), F32),
            pltpu.VMEM((16, 32, 512), F32),
            pltpu.VMEM((8, 8, 512), F32),
            pltpu.VMEM((8, 512), F32),
            pltpu.VMEM((8, 512), F32),
            pltpu.SMEM((1,), jnp.int32),
            pltpu.SMEM((1,), jnp.int32),
            dma((len(PIECES),)),
            dma((4,)),
            dma((n,)),
            dma((n,)),
            dma((8,)),
            dma((8,)),
            dma((24,)),
            dma((24,)),
            dma((24,)),
            dma((24,)),
        ],
        compiler_params=pltpu.CompilerParams(
            collective_id=0, has_side_effects=True, vmem_limit_bytes=48 << 20
        ),
        name="outer_step",
    )(local_params.reshape(4, 2, 16, 32, 512), global_params, momentum, step_counts, alive)
    out, nm = pl.pallas_call(
        store,
        out_shape=(jax.ShapeDtypeStruct((4, 2, 16, 32, 512), F32), jax.ShapeDtypeStruct((32, 8192), F32)),
        in_specs=[pl.BlockSpec(memory_space=pltpu.VMEM)] * 2,
        out_specs=(hbm, hbm),
        scratch_shapes=[dma((9,))],
        compiler_params=pltpu.CompilerParams(vmem_limit_bytes=16 << 20),
        name="store",
    )(out, nm)
    return out.reshape(4096, 512), nm


def solution(mesh):
    in_specs = (
        P("worker", None, "fsdp"),
        P(("worker", "fsdp"), None),
        P(("worker", "fsdp"), None),
        P("worker"),
        P("worker"),
    )
    out_specs = (P(None, "fsdp"), P(("worker", "fsdp"), None))
    return jax.shard_map(local, mesh=mesh, in_specs=in_specs, out_specs=out_specs, check_vma=False)
```
